32 devices in a mesh: blk: 4 (over x, core), uly: 8 (over z, y).
Axes of the slice: x: 2, y: 2, z: 4, core: 2. Of those that a mesh axis runs over, the one named last changes fastest.
Arguments:
- video: bfloat16 [6144, 3072], P(('blk', 'uly')), may hold values from -6 to 6
- w_qkv: bfloat16 [3072, 3072], P(None, 'uly'), may hold values from -0.109375 to 0.109375
- w_out: bfloat16 [1024, 3072], P('uly'), may hold values from -0.5 to 0.5
- q_gain: float32 [128], replicated, may hold values from 0.6 to 12
- k_gain: float32 [128], replicated, may hold values from 0.6 to 12
- tile_blocks: int32 [96, 27], P('blk'), may hold values from 0 to 95, as said below
- tile_counts: int32 [96], P('blk'), may hold values from 1 to 27
Outputs:
- mixed: bfloat16 [6144, 3072], P(('blk', 'uly'))
The draws below stay inside these ranges and needn't reach their ends.
Inputs may be any that keep to these rules, and one draw needn't show every extreme that they name: `tile_blocks`: tile t's list holds distinct tiles whose frame, row and column tile coordinates each differ from t's by at most one, t itself among them, in the order of increasing offset (frame, then row, then column offset from -1 to 1); entries at positions tile_counts[t] and later equal t. Some tile's list is full in every draw.
All inputs are finite; a program needn't handle non-finite values.
Results may differ from the reference program's by a relative error of at most 0.009.
The reference program's roundings to bfloat16 on the way count: a program that leaves them out, or rounds other values in their place, can miss the bound.
Values may be sent and summed in bfloat16 or wider, within the bound.
A program may use at most 128 MiB of HBM per device.

```python
import jax
import jax.numpy as jnp
import numpy as np
from jax import lax

D = 3072
HD = 128
TILE = 4
MAXB = 27
HH = 16
WW = 24
HEADS = 8
BLOCK = 64
NTS = 24
NTILES = 96
TOKENS = 6144
N_BLK = 4


def tile_lists(key):
    base_key = jax.random.fold_in(key, 7)
    grid_rows = HH // TILE
    grid_cols = WW // TILE
    per_slab = grid_rows * grid_cols
    count_all = per_slab * N_BLK
    tile_index = jnp.arange(count_all, dtype=jnp.int32)
    tile_layer = tile_index // per_slab
    tile_rest = tile_index % per_slab
    tile_row = tile_rest // grid_cols
    tile_col = tile_rest % grid_cols
    offsets = np.array([(a, b, c) for a in (-1, 0, 1) for b in (-1, 0, 1) for c in (-1, 0, 1)], dtype=np.int32)
    near_layer = tile_layer[:, None] + offsets[None, :, 0]
    near_row = tile_row[:, None] + offsets[None, :, 1]
    near_col = tile_col[:, None] + offsets[None, :, 2]
    inside = (near_layer >= 0) & (near_layer < N_BLK) & (near_row >= 0) & (near_row < grid_rows) & (near_col >= 0) & (near_col < grid_cols)
    coin_flips = jax.random.randint(jax.random.fold_in(base_key, 1), (count_all, 27), 0, 2)
    pick_layer = jax.random.randint(jax.random.fold_in(base_key, 2), (), 1, N_BLK - 1)
    pick_row = jax.random.randint(jax.random.fold_in(base_key, 3), (), 1, grid_rows - 1)
    pick_col = jax.random.randint(jax.random.fold_in(base_key, 4), (), 1, grid_cols - 1)
    chosen = pick_layer * per_slab + pick_row * grid_cols + pick_col
    own_slot = jnp.arange(27, dtype=jnp.int32) == 13
    kept_mask = inside & ((coin_flips == 1) | own_slot[None, :] | (tile_index == chosen)[:, None])
    block_ids = near_layer * per_slab + near_row * grid_cols + near_col
    block_ids = jnp.where(kept_mask, block_ids, tile_index[:, None])
    sort_keys = jnp.where(kept_mask, 0, 27) + jnp.arange(27, dtype=jnp.int32)[None, :]
    sort_order = jnp.argsort(sort_keys, axis=1)
    listed = jnp.take_along_axis(block_ids, sort_order, axis=1).astype(jnp.int32)
    counts = jnp.sum(kept_mask.astype(jnp.int32), axis=1).astype(jnp.int32)
    return (listed, counts)


def draw_tile_blocks(key, part):
    return tile_lists(key)[0]


def draw_tile_counts(key, part):
    return tile_lists(key)[1]


def gain_values(key, salt):
    spread = jax.random.uniform(jax.random.fold_in(key, salt), (HD,), minval=-0.5, maxval=0.8)
    values_out = jnp.exp(spread)
    return values_out.astype(jnp.float32)


def draw_q_gain(key, part):
    return gain_values(key, 21)


def draw_k_gain(key, part):
    return gain_values(key, 31)


def steps_of(stream_key, extent, shards, low, top_value):
    loudness, own = 1.0, jax.random.fold_in(stream_key, 6)
    for dim, blocks in shards:
        heights = jnp.exp(jax.random.uniform(jax.random.fold_in(own, dim), (blocks,), jnp.float32, low / len(shards), top_value / len(shards)))
        loudness = loudness * jnp.repeat(heights, extent[dim] // blocks).reshape([-1 if axis == dim else 1 for axis in range(len(extent))])
    return loudness


def scatter_about(stream_key, dims, width, reach, shards=(), kind=jnp.bfloat16):
    level = steps_of(stream_key, dims, shards, -0.22, 0.18) if shards else 1.0
    values = jax.random.normal(stream_key, dims, jnp.float32) * width * level
    return jnp.minimum(jnp.maximum(values, -reach), reach).astype(kind)


def setup_inputs(seed: int = 0) -> dict:
    seeds = jax.random.split(jax.random.key(seed), 8)
    video = scatter_about(seeds[0], (TOKENS, D), 1.0, 6.0, ((0, 32),))
    w_qkv = scatter_about(seeds[1], (D, HEADS * 3 * HD), D ** -0.5, 0.109375, ((1, 8),))
    w_out = scatter_about(seeds[2], (HEADS * HD, D), HD ** -0.5, 0.5, ((0, 8),))
    q_gain = draw_q_gain(jax.random.fold_in(seeds[7], 71), 0)
    k_gain = draw_k_gain(jax.random.fold_in(seeds[7], 71), 0)
    tile_blocks = draw_tile_blocks(jax.random.fold_in(seeds[7], 71), 0)
    tile_counts = draw_tile_counts(jax.random.fold_in(seeds[7], 71), 0)
    return {"video": video, "w_qkv": w_qkv, "w_out": w_out, "q_gain": q_gain, "k_gain": k_gain, "tile_blocks": tile_blocks, "tile_counts": tile_counts}


def norm_rows(values_in, gain):
    return values_in * lax.rsqrt(lax.optimization_barrier(jnp.mean(values_in * values_in, axis=-1, keepdims=True)) + 1e-06) * gain

def attend_tiles(query_tiles, gathered, live_keys):
    key_part = gathered[..., :HD].astype(jnp.float32)
    value_part = gathered[..., HD:].astype(jnp.float32)
    scores = jnp.einsum('tqd,tkd->tqk', query_tiles.astype(jnp.float32), key_part)
    scores = jnp.where(live_keys[:, None, :], scores, -jnp.inf)
    largest = lax.optimization_barrier(jnp.max(scores, axis=-1, keepdims=True))
    weights = jnp.exp(scores - largest)
    running = lax.optimization_barrier(jnp.sum(weights, axis=-1, keepdims=True))
    rounded = lax.optimization_barrier(weights.astype(jnp.bfloat16)).astype(jnp.float32)
    summed = jnp.einsum('tqk,tkd->tqd', rounded, value_part)
    return (summed / running).astype(jnp.bfloat16)

def reference(video, w_qkv, w_out, q_gain, k_gain, tile_blocks, tile_counts):
    slot_index = jnp.arange(MAXB).astype(jnp.int32)
    live_keys = jnp.repeat(slot_index[None, :] < tile_counts[:, None], BLOCK, axis=1)

    def one_head(running, head):
        columns = lax.dynamic_slice_in_dim(w_qkv, head * 3 * HD, 3 * HD, 1)
        projected = jnp.dot(video, columns, preferred_element_type=jnp.float32)
        queries = (norm_rows(projected[:, :HD], q_gain) * HD ** (-0.5)).astype(jnp.bfloat16)
        keys_now = norm_rows(projected[:, HD:2 * HD], k_gain).astype(jnp.bfloat16)
        values_now = projected[:, 2 * HD:].astype(jnp.bfloat16)
        key_value = jnp.concatenate([keys_now, values_now], axis=1).reshape(NTILES, BLOCK, 2 * HD)

        def one_slab(inputs):
            query_tiles, block_ids, live_now = inputs
            gathered = key_value[block_ids].reshape(NTS, MAXB * BLOCK, 2 * HD)
            return attend_tiles(query_tiles, gathered, live_now)
        attended = lax.map(one_slab, (queries.reshape(N_BLK, NTS, BLOCK, HD), tile_blocks.reshape(N_BLK, NTS, MAXB), live_keys.reshape(N_BLK, NTS, MAXB * BLOCK)))
        attended = attended.reshape(TOKENS, HD)
        row_block = lax.dynamic_slice_in_dim(w_out, head * HD, HD, 0)
        return (running + jnp.dot(attended, row_block, preferred_element_type=jnp.float32), None)
    start = jnp.zeros((TOKENS, D), jnp.float32)
    summed, _ = lax.scan(one_head, start, jnp.arange(HEADS).astype(jnp.int32))
    return summed.astype(jnp.bfloat16)
```

```python
import functools

import jax
import jax.numpy as jnp
from jax import lax
from jax.experimental import pallas as pl
from jax.experimental.pallas import tpu as pltpu
from jax.sharding import PartitionSpec as P

MAXB = 27
BLOCK = 64
CHUNK = 4
MESH = pl.DeviceIdType.MESH
ANY = pl.BlockSpec(memory_space=pl.ANY)


def remote(src, dst, send, recv, blk, uly):
    return pltpu.make_async_remote_copy(
        src_ref=src,
        dst_ref=dst,
        send_sem=send,
        recv_sem=recv,
        device_id=(blk, uly),
        device_id_type=MESH,
    )


def when(cond, fn):
    pl.when(cond)(fn)


def gather_kernel(
    groups,
    video,
    wq,
    wo,
    vid2,
    wq_all,
    wo_all,
    local_sem,
    vs,
    vr,
    zs,
    zr,
    xs,
    xr,
    cs,
    cr,
    ds,
    dr,
    ozs,
    ozr,
    oys,
    oyr,
    ocs,
    ocr,
    ods,
    odr,
):
    blk, uly = lax.axis_index("blk"), lax.axis_index("uly")
    a, y = uly // 2, uly % 2
    c, core = blk % 4, blk % 2
    x_c = c + 2 - 4 * (c // 2)
    xp = blk - c + x_c
    cp = blk + 1 - 2 * core
    yp = uly + 1 - 2 * y
    last = groups - 1
    rows = video.shape[0]
    part = wq.shape[0] // 4
    half = wo.shape[0] // 2

    barrier = pltpu.get_barrier_semaphore()

    def greet(b, u):
        pl.semaphore_signal(barrier, inc=1, device_id=(b, u), device_id_type=MESH)

    greet(xp, uly)
    greet(cp, uly)
    greet(blk, yp)
    when(a > 0, lambda: greet(blk, uly - 2))
    when(a < last, lambda: greet(blk, uly + 2))
    pl.semaphore_wait(barrier, 3 + (a > 0).astype(jnp.int32) + (a < last).astype(jnp.int32))

    def q_at(s, piece):
        return wq_all.at[s, pl.ds(pl.multiple_of(piece * part, 16), part)]

    def o_at(s, side):
        return wo_all.at[s, pl.ds(pl.multiple_of(side * half, 16), half)]

    q_own = wq.at[pl.ds(pl.multiple_of(c * part, 16), part)]
    o_own = wo.at[pl.ds(pl.multiple_of(core * half, 16), half)]
    v_dst = vid2.at[pl.ds(pl.multiple_of(y * rows, 16), rows)]
    v_peer = vid2.at[pl.ds(pl.multiple_of((1 - y) * rows, 16), rows)]

    onward = (uly + 2, uly - 2)
    can_go = (a < last, a > 0)

    def has(d, t):
        return (a >= t) if d == 0 else (a + t <= last)

    def came(d, t):
        return (a - t) if d == 0 else (a + t)

    def goes(d, t):
        return jnp.logical_and(has(d, t), can_go[d])

    for d in range(2):
        when(
            can_go[d],
            lambda d=d: remote(
                q_own, q_at(a, c), zs.at[d, 0], zr.at[d, 0], blk, onward[d]
            ).start(),
        )
    v_copy = remote(video, v_dst, vs, vr, blk, yp)
    v_copy.start()
    mine = [
        pltpu.make_async_copy(wq, wq_all.at[a], local_sem.at[0]),
        pltpu.make_async_copy(video, v_dst, local_sem.at[1]),
        pltpu.make_async_copy(wo, wo_all.at[uly], local_sem.at[2]),
    ]
    for copy in mine:
        copy.start()

    def q_on(d, t):
        return remote(
            q_at(came(d, t), c), q_at(came(d, t), c), zs.at[d, t], zr.at[d, t], blk, onward[d]
        )

    def q_x(d, t):
        r = q_at(came(d, t), c)
        return remote(r, r, xs.at[d, t - 1], xr.at[d, t - 1], xp, uly)

    def q_c(d, t):
        r = q_at(came(d, t), c)
        return remote(r, r, cs.at[d, t - 1], cr.at[d, t - 1], cp, uly)

    def q_d(d, t):
        r = q_at(came(d, t), x_c)
        return remote(r, r, ds.at[d, t - 1], dr.at[d, t - 1], cp, uly)

    def q_in(d, t):
        r = q_at(came(d, t), c)
        return remote(r, r, zs.at[d, t - 1], zr.at[d, t - 1], blk, yp)

    def q_xin(d, t):
        r = q_at(came(d, t), x_c)
        return remote(r, r, xs.at[d, t - 1], xr.at[d, t - 1], xp, uly)

    def q_cin(d, t, piece, s, r):
        ref = q_at(came(d, t), piece)
        return remote(ref, ref, s.at[d, t - 1], r.at[d, t - 1], cp, uly)

    def arrive(d, t):
        q_in(d, t).wait_recv()
        if t < last:
            when(can_go[d], lambda: q_on(d, t).start())
        q_x(d, t).start()
        q_c(d, t).start()

    def cross(d, t):
        q_xin(d, t).wait_recv()
        q_d(d, t).start()

    for t in range(1, last + 1):
        for d in range(2):
            when(has(d, t), lambda d=d, t=t: arrive(d, t))
        if t > 1:
            for d in range(2):
                when(has(d, t - 1), lambda d=d, t=t: cross(d, t - 1))

    def o_slot(d, t, side=None):
        return came(d, t) * 2 + (y if side is None else side)

    def o_on(d, t):
        src = o_own if t == 0 else o_at(o_slot(d, t), core)
        return remote(
            src, o_at(o_slot(d, t), core), ozs.at[d, t], ozr.at[d, t], blk, onward[d]
        )

    def o_in(d, t):
        r = o_at(o_slot(d, t), core)
        return remote(r, r, ozs.at[d, t - 1], ozr.at[d, t - 1], blk, yp)

    def o_y(d, t):
        src = o_own if t == 0 else o_at(o_slot(d, t), core)
        return remote(src, o_at(o_slot(d, t), core), oys.at[d, t], oyr.at[d, t], blk, yp)

    def o_yin(d, t):
        r = o_at(o_slot(d, t, 1 - y), core)
        return remote(r, r, oys.at[d, t], oyr.at[d, t], blk, yp)

    def o_c(d, t):
        r = o_at(o_slot(d, t), core)
        return remote(r, r, ocs.at[d, t - 1], ocr.at[d, t - 1], cp, uly)

    def o_d(d, t):
        r = o_at(o_slot(d, t, 1 - y), core)
        return remote(r, r, ods.at[d, t], odr.at[d, t], cp, uly)

    def o_cin(d, t):
        r = o_at(o_slot(d, t), 1 - core)
        return remote(r, r, ocs.at[d, t - 1], ocr.at[d, t - 1], cp, uly)

    def o_din(d, t):
        r = o_at(o_slot(d, t, 1 - y), 1 - core)
        return remote(r, r, ods.at[d, t], odr.at[d, t], cp, uly)

    def o_arrive(d, t):
        o_in(d, t).wait_recv()
        if t < last:
            when(can_go[d], lambda: o_on(d, t).start())
        o_y(d, t).start()
        o_c(d, t).start()

    def o_cross(d, t):
        o_yin(d, t).wait_recv()
        o_d(d, t).start()

    for d in range(2):
        when(can_go[d], lambda d=d: o_on(d, 0).start())
    o_y(0, 0).start()
    if last > 0:
        for d in range(2):
            when(has(d, last), lambda d=d: cross(d, last))
    for t in range(1, last + 1):
        for d in range(2):
            when(has(d, t), lambda d=d, t=t: o_arrive(d, t))
        if t == 1:
            o_cross(0, 0)
        else:
            for d in range(2):
                when(has(d, t - 1), lambda d=d, t=t: o_cross(d, t - 1))
    for d in range(2):
        when(has(d, last), lambda d=d: o_cross(d, last))

    for copy in mine:
        copy.wait()
    v_copy.wait_send()
    remote(video, v_peer, vs, vr, blk, yp).wait_recv()
    o_y(0, 0).wait_send()
    o_d(0, 0).wait_send()
    o_din(0, 0).wait_recv()
    for d in range(2):
        when(
            can_go[d],
            lambda d=d: remote(
                q_own, q_at(a, c), zs.at[d, 0], zr.at[d, 0], blk, onward[d]
            ).wait_send(),
        )
        when(can_go[d], lambda d=d: o_on(d, 0).wait_send())

        def finish(d, t):
            if t < last:
                when(can_go[d], lambda: q_on(d, t).wait_send())
                when(can_go[d], lambda: o_on(d, t).wait_send())
            q_x(d, t).wait_send()
            q_c(d, t).wait_send()
            q_d(d, t).wait_send()
            q_cin(d, t, c + 1 - 2 * core, cs, cr).wait_recv()
            q_cin(d, t, x_c + 1 - 2 * core, ds, dr).wait_recv()
            o_y(d, t).wait_send()
            o_c(d, t).wait_send()
            o_d(d, t).wait_send()
            o_cin(d, t).wait_recv()
            o_din(d, t).wait_recv()

        for t in range(1, last + 1):
            when(has(d, t), lambda d=d, t=t: finish(d, t))


def gather_weights(video, wq, wo, groups):
    rows = video.shape[0]
    pair = pltpu.SemaphoreType.DMA((2, groups))
    return pl.pallas_call(
        functools.partial(gather_kernel, groups),
        out_shape=(
            jax.ShapeDtypeStruct((2 * rows, video.shape[1]), video.dtype),
            jax.ShapeDtypeStruct((groups,) + wq.shape, wq.dtype),
            jax.ShapeDtypeStruct((2 * groups,) + wo.shape, wo.dtype),
        ),
        in_specs=[ANY] * 3,
        out_specs=(ANY,) * 3,
        scratch_shapes=[
            pltpu.SemaphoreType.DMA((3,)),
            pltpu.SemaphoreType.DMA,
            pltpu.SemaphoreType.DMA,
        ]
        + [pair] * 16,
        compiler_params=pltpu.CompilerParams(collective_id=0, has_side_effects=True),
    )(video, wq, wo)


def exchange_kernel(groups, slabs, q, kv, q_all, kv_all, local_sem, qs, qr, ks, kr, ps, pr, ns, nr):
    blk, uly = lax.axis_index("blk"), lax.axis_index("uly")
    a, y = uly // 2, uly % 2
    has_prev, has_next = blk > 0, blk < slabs - 1

    barrier = pltpu.get_barrier_semaphore()

    def greet(b, u):
        pl.semaphore_signal(barrier, inc=1, device_id=(b, u), device_id_type=MESH)

    for k in range(1, groups):
        greet(blk, ((a + k) % groups) * 2 + y)
    when(has_prev, lambda: greet(blk - 1, uly))
    when(has_next, lambda: greet(blk + 1, uly))
    pl.semaphore_wait(
        barrier, groups - 1 + has_prev.astype(jnp.int32) + has_next.astype(jnp.int32)
    )

    def there(k):
        return (a + k) % groups

    def source(k):
        return (a - k + groups) % groups

    def kv_out(k):
        return remote(
            kv.at[there(k)], kv_all.at[1, a], ks.at[k], kr.at[k], blk, there(k) * 2 + y
        )

    def q_out(k):
        return remote(q.at[there(k)], q_all.at[a], qs.at[k], qr.at[k], blk, there(k) * 2 + y)

    def kv_in(k):
        r = kv_all.at[1, source(k)]
        return remote(r, r, ks.at[k], kr.at[k], blk, there(k) * 2 + y)

    def q_in(k):
        r = q_all.at[source(k)]
        return remote(r, r, qs.at[k], qr.at[k], blk, there(k) * 2 + y)

    def to_prev(k):
        src = kv.at[a] if k == 0 else kv_all.at[1, source(k)]
        return remote(src, kv_all.at[2, source(k)], ps.at[k], pr.at[k], blk - 1, uly)

    def to_next(k):
        src = kv.at[a] if k == 0 else kv_all.at[1, source(k)]
        return remote(src, kv_all.at[0, source(k)], ns.at[k], nr.at[k], blk + 1, uly)

    def from_prev(k):
        r = kv_all.at[0, source(k)]
        return remote(r, r, ns.at[k], nr.at[k], blk - 1, uly)

    def from_next(k):
        r = kv_all.at[2, source(k)]
        return remote(r, r, ps.at[k], pr.at[k], blk + 1, uly)

    for k in range(1, groups):
        kv_out(k).start()
    when(has_prev, lambda: to_prev(0).start())
    when(has_next, lambda: to_next(0).start())
    mine = [
        pltpu.make_async_copy(q.at[a], q_all.at[a], local_sem.at[0]),
        pltpu.make_async_copy(kv.at[a], kv_all.at[1, a], local_sem.at[1]),
    ]
    for copy in mine:
        copy.start()
    for k in range(1, groups):
        q_out(k).start()
    for k in range(1, groups):
        kv_in(k).wait_recv()
        when(has_prev, lambda k=k: to_prev(k).start())
        when(has_next, lambda k=k: to_next(k).start())
    for copy in mine:
        copy.wait()
    for k in range(1, groups):
        kv_out(k).wait_send()
        q_out(k).wait_send()
        q_in(k).wait_recv()
    for k in range(groups):

        def prev_done(k=k):
            to_prev(k).wait_send()
            from_prev(k).wait_recv()

        def next_done(k=k):
            to_next(k).wait_send()
            from_next(k).wait_recv()

        when(has_prev, prev_done)
        when(has_next, next_done)


def exchange_heads(q, kv, groups, slabs):
    sems = pltpu.SemaphoreType.DMA((groups,))
    return pl.pallas_call(
        functools.partial(exchange_kernel, groups, slabs),
        out_shape=(
            jax.ShapeDtypeStruct(q.shape, q.dtype),
            jax.ShapeDtypeStruct((3,) + kv.shape, kv.dtype),
        ),
        in_specs=[ANY] * 2,
        out_specs=(ANY,) * 2,
        scratch_shapes=[pltpu.SemaphoreType.DMA((2,))] + [sems] * 8,
        compiler_params=pltpu.CompilerParams(collective_id=1, has_side_effects=True),
    )(q, kv)


def attend_kernel(head_size, ids, counts, q_ref, kv_ref, out_ref, keys):
    t = pl.program_id(0)
    count = counts[t]
    chunks = (count + CHUNK - 1) // CHUNK
    slots = ids.shape[1]

    def run(n):
        width = n * CHUNK * BLOCK
        for s in range(n * CHUNK):
            tile = ids[t, s]
            keys[s * BLOCK : (s + 1) * BLOCK, :] = kv_ref[
                pl.ds(pl.multiple_of(tile * BLOCK, BLOCK), BLOCK), :
            ]
        scores = lax.dot_general(
            q_ref[...],
            keys[:width, :head_size],
            (((1,), (1,)), ((), ())),
            preferred_element_type=jnp.float32,
        )
        column = lax.broadcasted_iota(jnp.int32, scores.shape, 1)
        scores = jnp.where(column < count * BLOCK, scores, -jnp.inf)
        largest = jnp.max(scores, axis=-1, keepdims=True)
        weights = jnp.exp(scores - largest)
        total = jnp.sum(weights, axis=-1, keepdims=True)
        summed = jnp.dot(
            weights.astype(jnp.bfloat16),
            keys[:width, head_size:],
            preferred_element_type=jnp.float32,
        )
        out_ref[...] = (summed / total).astype(jnp.bfloat16)

    for n in range(1, slots // CHUNK + 1):
        when(chunks == n, lambda n=n: run(n))


def attend(q, kv, ids, counts):
    rows, head_size = q.shape
    return pl.pallas_call(
        functools.partial(attend_kernel, head_size),
        out_shape=jax.ShapeDtypeStruct(q.shape, jnp.bfloat16),
        grid_spec=pltpu.PrefetchScalarGridSpec(
            num_scalar_prefetch=2,
            grid=(rows // BLOCK,),
            in_specs=[
                pl.BlockSpec((BLOCK, head_size), lambda t, i, n: (t, 0)),
                pl.BlockSpec(kv.shape, lambda t, i, n: (0, 0)),
            ],
            out_specs=pl.BlockSpec((BLOCK, head_size), lambda t, i, n: (t, 0)),
            scratch_shapes=[pltpu.VMEM((ids.shape[1] * BLOCK, 2 * head_size), jnp.bfloat16)],
        ),
        compiler_params=pltpu.CompilerParams(vmem_limit_bytes=32 << 20),
    )(ids, counts, q, kv)


def norm_rows(values_in, gain):
    return (
        values_in
        * lax.rsqrt(jnp.mean(values_in * values_in, axis=-1, keepdims=True) + 1e-06)
        * gain
    )


def local(video, w_qkv, w_out, q_gain, k_gain, tile_blocks, tile_counts):
    head_size = w_out.shape[0]
    ranks, slabs = lax.axis_size("uly"), lax.axis_size("blk")
    groups = ranks // 2
    slab_rows = video.shape[0] * ranks
    tiles = slab_rows // BLOCK
    rows2, w_all, wo_all = gather_weights(video, w_qkv, w_out, groups)
    projected = jnp.einsum("td,adn->atn", rows2, w_all, preferred_element_type=jnp.float32)
    queries = (norm_rows(projected[..., :head_size], q_gain) * head_size ** (-0.5)).astype(
        jnp.bfloat16
    )
    keys_now = norm_rows(projected[..., head_size : 2 * head_size], k_gain).astype(jnp.bfloat16)
    values_now = projected[..., 2 * head_size :].astype(jnp.bfloat16)
    key_value = jnp.concatenate([keys_now, values_now], axis=-1)
    q_all, kv_all = exchange_heads(queries, key_value, groups, slabs)
    local_ids = tile_blocks - (lax.axis_index("blk") - 1) * tiles
    slots = -(-MAXB // CHUNK) * CHUNK
    local_ids = jnp.concatenate([local_ids] + [local_ids[:, -1:]] * (slots - MAXB), axis=1)
    attended = attend(
        q_all.reshape(slab_rows, head_size),
        kv_all.reshape(3 * slab_rows, 2 * head_size),
        local_ids,
        tile_counts,
    )
    by_token = lax.all_to_all(
        attended.reshape(ranks, video.shape[0], head_size), "uly", 0, 0, tiled=True
    )
    by_token = by_token.transpose(1, 0, 2).reshape(video.shape[0], ranks * head_size)
    mixed = jnp.dot(
        by_token,
        wo_all.reshape(ranks * head_size, w_out.shape[1]),
        preferred_element_type=jnp.float32,
    )
    return mixed.astype(jnp.bfloat16)


def solution(mesh):
    return jax.shard_map(
        local,
        mesh=mesh,
        in_specs=(
            P(("blk", "uly"), None),
            P(None, "uly"),
            P("uly", None),
            P(),
            P(),
            P("blk", None),
            P("blk"),
        ),
        out_specs=P(("blk", "uly"), None),
        check_vma=False,
    )
```

```python
import functools

import jax
import jax.numpy as jnp
from jax import lax
from jax.experimental import pallas as pl
from jax.experimental.pallas import tpu as pltpu
from jax.sharding import PartitionSpec as P

MAXB = 27
BLOCK = 64
CHUNK = 4
Q_PARTS = 4
O_PARTS = 2
V_PARTS = 2
MESH = pl.DeviceIdType.MESH
ANY = pl.BlockSpec(memory_space=pl.ANY)


def remote(src, dst, send, recv, blk, uly):
    return pltpu.make_async_remote_copy(
        src_ref=src,
        dst_ref=dst,
        send_sem=send,
        recv_sem=recv,
        device_id=(blk, uly),
        device_id_type=MESH,
    )


def when(cond, fn):
    pl.when(cond)(fn)


def gather_kernel(
    groups,
    video,
    wq,
    wo,
    vid2,
    wq_all,
    wo_all,
    local_sem,
    vs,
    vr,
    zs,
    zr,
    xs,
    xr,
    cs,
    cr,
    ds,
    dr,
    ozs,
    ozr,
    oys,
    oyr,
    ocs,
    ocr,
    ods,
    odr,
):
    blk, uly = lax.axis_index("blk"), lax.axis_index("uly")
    a, y = uly // 2, uly % 2
    c, core = blk % 4, blk % 2
    x_c = c + 2 - 4 * (c // 2)
    xp = blk - c + x_c
    cp = blk + 1 - 2 * core
    yp = uly + 1 - 2 * y
    last = groups - 1
    rows = video.shape[0]
    part = wq.shape[0] // 4
    half = wo.shape[0] // 2

    barrier = pltpu.get_barrier_semaphore()

    def greet(b, u):
        pl.semaphore_signal(barrier, inc=1, device_id=(b, u), device_id_type=MESH)

    greet(xp, uly)
    greet(cp, uly)
    greet(blk, yp)
    when(a > 0, lambda: greet(blk, uly - 2))
    when(a < last, lambda: greet(blk, uly + 2))
    pl.semaphore_wait(barrier, 3 + (a > 0).astype(jnp.int32) + (a < last).astype(jnp.int32))

    q_sub, o_sub = part // Q_PARTS, half // O_PARTS

    def q_at(s, piece, p):
        return wq_all.at[s, pl.ds(pl.multiple_of(piece * part + p * q_sub, 16), q_sub)]

    def o_at(s, side, p):
        return wo_all.at[s, pl.ds(pl.multiple_of(side * half + p * o_sub, 16), o_sub)]

    def q_own(p):
        return wq.at[pl.ds(pl.multiple_of(c * part + p * q_sub, 16), q_sub)]

    def o_own(p):
        return wo.at[pl.ds(pl.multiple_of(core * half + p * o_sub, 16), o_sub)]

    v_sub = rows // V_PARTS

    def v_out(p):
        src = video.at[pl.ds(p * v_sub, v_sub)]
        dst = vid2.at[pl.ds(pl.multiple_of(y * rows + p * v_sub, 16), v_sub)]
        return remote(src, dst, vs.at[p], vr.at[p], blk, yp)

    def v_in(p):
        r = vid2.at[pl.ds(pl.multiple_of((1 - y) * rows + p * v_sub, 16), v_sub)]
        return remote(r, r, vs.at[p], vr.at[p], blk, yp)

    onward = (uly + 2, uly - 2)
    can_go = (a < last, a > 0)

    def has(d, t):
        return (a >= t) if d == 0 else (a + t <= last)

    def came(d, t):
        return (a - t) if d == 0 else (a + t)

    def q_on(d, t, p):
        dst = q_at(came(d, t), c, p)
        k = t * Q_PARTS + p
        return remote(q_own(p) if t == 0 else dst, dst, zs.at[d, k], zr.at[d, k], blk, onward[d])

    def q_copy(d, t, p, piece, send, recv, to_blk, to_uly):
        r = q_at(came(d, t), piece, p)
        k = (t - 1) * Q_PARTS + p
        return remote(r, r, send.at[d, k], recv.at[d, k], to_blk, to_uly)

    def q_in(d, t, p):
        return q_copy(d, t, p, c, zs, zr, blk, yp)

    def q_x(d, t, p):
        return q_copy(d, t, p, c, xs, xr, xp, uly)

    def q_xin(d, t, p):
        return q_copy(d, t, p, x_c, xs, xr, xp, uly)

    def q_c(d, t, p):
        return q_copy(d, t, p, c, cs, cr, cp, uly)

    def q_cin(d, t, p):
        return q_copy(d, t, p, c + 1 - 2 * core, cs, cr, cp, uly)

    def q_d(d, t, p):
        return q_copy(d, t, p, x_c, ds, dr, cp, uly)

    def q_din(d, t, p):
        return q_copy(d, t, p, x_c + 1 - 2 * core, ds, dr, cp, uly)

    def o_copy(d, t, p, slot, side, send, recv, to_blk, to_uly, own=False):
        r = o_at(slot, side, p)
        k = t * O_PARTS + p
        return remote(o_own(p) if own else r, r, send.at[d, k], recv.at[d, k], to_blk, to_uly)

    def o_on(d, t, p):
        return o_copy(d, t, p, came(d, t) * 2 + y, core, ozs, ozr, blk, onward[d], t == 0)

    def o_in(d, t, p):
        return o_copy(d, t - 1, p, came(d, t) * 2 + y, core, ozs, ozr, blk, yp)

    def o_y(d, t, p):
        return o_copy(d, t, p, came(d, t) * 2 + y, core, oys, oyr, blk, yp, t == 0)

    def o_yin(d, t, p):
        return o_copy(d, t, p, came(d, t) * 2 + 1 - y, core, oys, oyr, blk, yp)

    def o_c(d, t, p):
        return o_copy(d, t, p, came(d, t) * 2 + y, core, ocs, ocr, cp, uly)

    def o_cin(d, t, p):
        return o_copy(d, t, p, came(d, t) * 2 + y, 1 - core, ocs, ocr, cp, uly)

    def o_d(d, t, p):
        return o_copy(d, t, p, came(d, t) * 2 + 1 - y, core, ods, odr, cp, uly)

    def o_din(d, t, p):
        return o_copy(d, t, p, came(d, t) * 2 + 1 - y, 1 - core, ods, odr, cp, uly)

    def q_arrive(d, t, p):
        q_in(d, t, p).wait_recv()
        if t < last:
            when(can_go[d], lambda: q_on(d, t, p).start())
        q_x(d, t, p).start()
        q_c(d, t, p).start()

    def q_cross(d, t, p):
        q_xin(d, t, p).wait_recv()
        q_d(d, t, p).start()

    def o_arrive(d, t, p):
        o_in(d, t, p).wait_recv()
        if t < last:
            when(can_go[d], lambda: o_on(d, t, p).start())
        o_y(d, t, p).start()
        o_c(d, t, p).start()

    def o_cross(d, t, p):
        o_yin(d, t, p).wait_recv()
        o_d(d, t, p).start()

    def each(cond, parts, fn):
        def body():
            for p in range(parts):
                fn(p)

        when(cond, body)

    for p in range(Q_PARTS):
        for d in range(2):
            when(can_go[d], lambda d=d, p=p: q_on(d, 0, p).start())
    for p in range(V_PARTS):
        v_out(p).start()
    for p in range(O_PARTS):
        o_y(0, 0, p).start()
    mine = [
        pltpu.make_async_copy(wq, wq_all.at[a], local_sem.at[0]),
        pltpu.make_async_copy(
            video, vid2.at[pl.ds(pl.multiple_of(y * rows, 16), rows)], local_sem.at[1]
        ),
        pltpu.make_async_copy(wo, wo_all.at[uly], local_sem.at[2]),
    ]
    for copy in mine:
        copy.start()

    for t in range(1, last + 1):
        for p in range(Q_PARTS):
            for d in range(2):
                when(has(d, t), lambda d=d, p=p, t=t: q_arrive(d, t, p))
            if t > 1:
                for d in range(2):
                    when(has(d, t - 1), lambda d=d, p=p, t=t: q_cross(d, t - 1, p))
        if t == last:
            for p in range(O_PARTS):
                for d in range(2):
                    when(can_go[d], lambda d=d, p=p: o_on(d, 0, p).start())
    for p in range(O_PARTS):
        o_cross(0, 0, p)
    for d in range(2):
        each(has(d, last), Q_PARTS, lambda p, d=d: q_cross(d, last, p))
    for t in range(1, last + 1):
        for p in range(O_PARTS):
            for d in range(2):
                when(has(d, t), lambda d=d, p=p, t=t: o_arrive(d, t, p))
            if t > 1:
                for d in range(2):
                    when(has(d, t - 1), lambda d=d, p=p, t=t: o_cross(d, t - 1, p))
    for d in range(2):
        each(has(d, last), O_PARTS, lambda p, d=d: o_cross(d, last, p))

    for copy in mine:
        copy.wait()
    for p in range(V_PARTS):
        v_out(p).wait_send()
        v_in(p).wait_recv()
    for p in range(O_PARTS):
        o_y(0, 0, p).wait_send()
        o_d(0, 0, p).wait_send()
        o_din(0, 0, p).wait_recv()

    def q_end(d, t, p):
        q_x(d, t, p).wait_send()
        q_c(d, t, p).wait_send()
        q_d(d, t, p).wait_send()
        q_cin(d, t, p).wait_recv()
        q_din(d, t, p).wait_recv()

    def o_end(d, t, p):
        o_y(d, t, p).wait_send()
        o_c(d, t, p).wait_send()
        o_d(d, t, p).wait_send()
        o_cin(d, t, p).wait_recv()
        o_din(d, t, p).wait_recv()

    for d in range(2):
        for t in range(last):
            on = can_go[d] if t == 0 else jnp.logical_and(has(d, t), can_go[d])
            each(on, Q_PARTS, lambda p, d=d, t=t: q_on(d, t, p).wait_send())
            each(on, O_PARTS, lambda p, d=d, t=t: o_on(d, t, p).wait_send())
        for t in range(1, last + 1):
            each(has(d, t), Q_PARTS, lambda p, d=d, t=t: q_end(d, t, p))
            each(has(d, t), O_PARTS, lambda p, d=d, t=t: o_end(d, t, p))


def gather_weights(video, wq, wo, groups):
    rows = video.shape[0]
    q_sems = pltpu.SemaphoreType.DMA((2, groups * Q_PARTS))
    o_sems = pltpu.SemaphoreType.DMA((2, groups * O_PARTS))
    return pl.pallas_call(
        functools.partial(gather_kernel, groups),
        out_shape=(
            jax.ShapeDtypeStruct((2 * rows, video.shape[1]), video.dtype),
            jax.ShapeDtypeStruct((groups,) + wq.shape, wq.dtype),
            jax.ShapeDtypeStruct((2 * groups,) + wo.shape, wo.dtype),
        ),
        in_specs=[ANY] * 3,
        out_specs=(ANY,) * 3,
        scratch_shapes=[
            pltpu.SemaphoreType.DMA((3,)),
            pltpu.SemaphoreType.DMA((V_PARTS,)),
            pltpu.SemaphoreType.DMA((V_PARTS,)),
        ]
        + [q_sems] * 8
        + [o_sems] * 8,
        compiler_params=pltpu.CompilerParams(collective_id=0, has_side_effects=True),
    )(video, wq, wo)


def exchange_kernel(groups, slabs, q, kv, q_all, kv_all, local_sem, qs, qr, ks, kr, ps, pr, ns, nr):
    blk, uly = lax.axis_index("blk"), lax.axis_index("uly")
    a, y = uly // 2, uly % 2
    has_prev, has_next = blk > 0, blk < slabs - 1

    barrier = pltpu.get_barrier_semaphore()

    def greet(b, u):
        pl.semaphore_signal(barrier, inc=1, device_id=(b, u), device_id_type=MESH)

    for k in range(1, groups):
        greet(blk, ((a + k) % groups) * 2 + y)
    when(has_prev, lambda: greet(blk - 1, uly))
    when(has_next, lambda: greet(blk + 1, uly))
    pl.semaphore_wait(
        barrier, groups - 1 + has_prev.astype(jnp.int32) + has_next.astype(jnp.int32)
    )

    def there(k):
        return (a + k) % groups

    def source(k):
        return (a - k + groups) % groups

    def kv_out(k):
        return remote(
            kv.at[there(k)], kv_all.at[1, a], ks.at[k], kr.at[k], blk, there(k) * 2 + y
        )

    def q_out(k):
        return remote(q.at[there(k)], q_all.at[a], qs.at[k], qr.at[k], blk, there(k) * 2 + y)

    def kv_in(k):
        r = kv_all.at[1, source(k)]
        return remote(r, r, ks.at[k], kr.at[k], blk, there(k) * 2 + y)

    def q_in(k):
        r = q_all.at[source(k)]
        return remote(r, r, qs.at[k], qr.at[k], blk, there(k) * 2 + y)

    def to_prev(k):
        src = kv.at[a] if k == 0 else kv_all.at[1, source(k)]
        return remote(src, kv_all.at[2, source(k)], ps.at[k], pr.at[k], blk - 1, uly)

    def to_next(k):
        src = kv.at[a] if k == 0 else kv_all.at[1, source(k)]
        return remote(src, kv_all.at[0, source(k)], ns.at[k], nr.at[k], blk + 1, uly)

    def from_prev(k):
        r = kv_all.at[0, source(k)]
        return remote(r, r, ns.at[k], nr.at[k], blk - 1, uly)

    def from_next(k):
        r = kv_all.at[2, source(k)]
        return remote(r, r, ps.at[k], pr.at[k], blk + 1, uly)

    for k in range(1, groups):
        kv_out(k).start()
    when(has_prev, lambda: to_prev(0).start())
    when(has_next, lambda: to_next(0).start())
    mine = [
        pltpu.make_async_copy(q.at[a], q_all.at[a], local_sem.at[0]),
        pltpu.make_async_copy(kv.at[a], kv_all.at[1, a], local_sem.at[1]),
    ]
    for copy in mine:
        copy.start()
    for k in range(1, groups):
        q_out(k).start()
    for k in range(1, groups):
        kv_in(k).wait_recv()
        when(has_prev, lambda k=k: to_prev(k).start())
        when(has_next, lambda k=k: to_next(k).start())
    for copy in mine:
        copy.wait()
    for k in range(1, groups):
        kv_out(k).wait_send()
        q_out(k).wait_send()
        q_in(k).wait_recv()
    for k in range(groups):

        def prev_done(k=k):
            to_prev(k).wait_send()
            from_prev(k).wait_recv()

        def next_done(k=k):
            to_next(k).wait_send()
            from_next(k).wait_recv()

        when(has_prev, prev_done)
        when(has_next, next_done)


def exchange_heads(q, kv, groups, slabs):
    sems = pltpu.SemaphoreType.DMA((groups,))
    return pl.pallas_call(
        functools.partial(exchange_kernel, groups, slabs),
        out_shape=(
            jax.ShapeDtypeStruct(q.shape, q.dtype),
            jax.ShapeDtypeStruct((3,) + kv.shape, kv.dtype),
        ),
        in_specs=[ANY] * 2,
        out_specs=(ANY,) * 2,
        scratch_shapes=[pltpu.SemaphoreType.DMA((2,))] + [sems] * 8,
        compiler_params=pltpu.CompilerParams(collective_id=1, has_side_effects=True),
    )(q, kv)


def attend_kernel(head_size, ids, counts, q_ref, kv_ref, out_ref, keys):
    t = pl.program_id(0)
    count = counts[t]
    chunks = (count + CHUNK - 1) // CHUNK
    slots = ids.shape[1]

    def run(n):
        width = n * CHUNK * BLOCK
        for s in range(n * CHUNK):
            tile = ids[t, s]
            keys[s * BLOCK : (s + 1) * BLOCK, :] = kv_ref[
                pl.ds(pl.multiple_of(tile * BLOCK, BLOCK), BLOCK), :
            ]
        scores = lax.dot_general(
            q_ref[...],
            keys[:width, :head_size],
            (((1,), (1,)), ((), ())),
            preferred_element_type=jnp.float32,
        )
        column = lax.broadcasted_iota(jnp.int32, scores.shape, 1)
        scores = jnp.where(column < count * BLOCK, scores, -jnp.inf)
        largest = jnp.max(scores, axis=-1, keepdims=True)
        weights = jnp.exp(scores - largest)
        total = jnp.sum(weights, axis=-1, keepdims=True)
        summed = jnp.dot(
            weights.astype(jnp.bfloat16),
            keys[:width, head_size:],
            preferred_element_type=jnp.float32,
        )
        out_ref[...] = (summed / total).astype(jnp.bfloat16)

    for n in range(1, slots // CHUNK + 1):
        when(chunks == n, lambda n=n: run(n))


def attend(q, kv, ids, counts):
    rows, head_size = q.shape
    return pl.pallas_call(
        functools.partial(attend_kernel, head_size),
        out_shape=jax.ShapeDtypeStruct(q.shape, jnp.bfloat16),
        grid_spec=pltpu.PrefetchScalarGridSpec(
            num_scalar_prefetch=2,
            grid=(rows // BLOCK,),
            in_specs=[
                pl.BlockSpec((BLOCK, head_size), lambda t, i, n: (t, 0)),
                pl.BlockSpec(kv.shape, lambda t, i, n: (0, 0)),
            ],
            out_specs=pl.BlockSpec((BLOCK, head_size), lambda t, i, n: (t, 0)),
            scratch_shapes=[pltpu.VMEM((ids.shape[1] * BLOCK, 2 * head_size), jnp.bfloat16)],
        ),
        compiler_params=pltpu.CompilerParams(vmem_limit_bytes=32 << 20),
    )(ids, counts, q, kv)


def norm_rows(values_in, gain):
    return (
        values_in
        * lax.rsqrt(jnp.mean(values_in * values_in, axis=-1, keepdims=True) + 1e-06)
        * gain
    )


def local(video, w_qkv, w_out, q_gain, k_gain, tile_blocks, tile_counts):
    head_size = w_out.shape[0]
    ranks, slabs = lax.axis_size("uly"), lax.axis_size("blk")
    groups = ranks // 2
    slab_rows = video.shape[0] * ranks
    tiles = slab_rows // BLOCK
    rows2, w_all, wo_all = gather_weights(video, w_qkv, w_out, groups)
    projected = jnp.einsum("td,adn->atn", rows2, w_all, preferred_element_type=jnp.float32)
    queries = (norm_rows(projected[..., :head_size], q_gain) * head_size ** (-0.5)).astype(
        jnp.bfloat16
    )
    keys_now = norm_rows(projected[..., head_size : 2 * head_size], k_gain).astype(jnp.bfloat16)
    values_now = projected[..., 2 * head_size :].astype(jnp.bfloat16)
    key_value = jnp.concatenate([keys_now, values_now], axis=-1)
    q_all, kv_all = exchange_heads(queries, key_value, groups, slabs)
    local_ids = tile_blocks - (lax.axis_index("blk") - 1) * tiles
    slots = -(-MAXB // CHUNK) * CHUNK
    local_ids = jnp.concatenate([local_ids] + [local_ids[:, -1:]] * (slots - MAXB), axis=1)
    attended = attend(
        q_all.reshape(slab_rows, head_size),
        kv_all.reshape(3 * slab_rows, 2 * head_size),
        local_ids,
        tile_counts,
    )
    by_token = lax.all_to_all(
        attended.reshape(ranks, video.shape[0], head_size), "uly", 0, 0, tiled=True
    )
    by_token = by_token.transpose(1, 0, 2).reshape(video.shape[0], ranks * head_size)
    mixed = jnp.dot(
        by_token,
        wo_all.reshape(ranks * head_size, w_out.shape[1]),
        preferred_element_type=jnp.float32,
    )
    return mixed.astype(jnp.bfloat16)


def solution(mesh):
    return jax.shard_map(
        local,
        mesh=mesh,
        in_specs=(
            P(("blk", "uly"), None),
            P(None, "uly"),
            P("uly", None),
            P(),
            P(),
            P("blk", None),
            P("blk"),
        ),
        out_specs=P(("blk", "uly"), None),
        check_vma=False,
    )
```

```python
import functools

import jax
import jax.numpy as jnp
from jax import lax
from jax.experimental import pallas as pl
from jax.experimental.pallas import tpu as pltpu
from jax.sharding import PartitionSpec as P

MAXB = 27
BLOCK = 64
CHUNK = 4
Q_PARTS = 4
O_PARTS = 2
V_PARTS = 2
MESH = pl.DeviceIdType.MESH
ANY = pl.BlockSpec(memory_space=pl.ANY)


def remote(src, dst, send, recv, blk, uly):
    return pltpu.make_async_remote_copy(
        src_ref=src,
        dst_ref=dst,
        send_sem=send,
        recv_sem=recv,
        device_id=(blk, uly),
        device_id_type=MESH,
    )


def through_vmem(sources, targets, rooms, sems):
    count = len(sources)
    ins = [pltpu.make_async_copy(sources[i], rooms[i], sems.at[i]) for i in range(count)]
    for copy in ins:
        copy.start()
    outs = []
    for i in range(count):
        ins[i].wait()
        outs.append(pltpu.make_async_copy(rooms[i], targets[i], sems.at[count + i]))
        outs[i].start()
    return outs


def when(cond, fn):
    pl.when(cond)(fn)


def gather_kernel(
    groups,
    video,
    wq,
    wo,
    vid2,
    wq_all,
    wo_all,
    local_sem,
    vs,
    vr,
    zs,
    zr,
    xs,
    xr,
    cs,
    cr,
    ds,
    dr,
    ozs,
    ozr,
    oys,
    oyr,
    ocs,
    ocr,
    ods,
    odr,
    wq_v,
    video_v,
    wo_v,
):
    blk, uly = lax.axis_index("blk"), lax.axis_index("uly")
    a, y = uly // 2, uly % 2
    c, core = blk % 4, blk % 2
    x_c = c + 2 - 4 * (c // 2)
    xp = blk - c + x_c
    cp = blk + 1 - 2 * core
    yp = uly + 1 - 2 * y
    last = groups - 1
    rows = video.shape[0]
    part = wq.shape[0] // 4
    half = wo.shape[0] // 2

    barrier = pltpu.get_barrier_semaphore()

    def greet(b, u):
        pl.semaphore_signal(barrier, inc=1, device_id=(b, u), device_id_type=MESH)

    greet(xp, uly)
    greet(cp, uly)
    greet(blk, yp)
    when(a > 0, lambda: greet(blk, uly - 2))
    when(a < last, lambda: greet(blk, uly + 2))
    pl.semaphore_wait(barrier, 3 + (a > 0).astype(jnp.int32) + (a < last).astype(jnp.int32))

    q_sub, o_sub = part // Q_PARTS, half // O_PARTS

    def q_at(s, piece, p):
        return wq_all.at[s, pl.ds(pl.multiple_of(piece * part + p * q_sub, 16), q_sub)]

    def o_at(s, side, p):
        return wo_all.at[s, pl.ds(pl.multiple_of(side * half + p * o_sub, 16), o_sub)]

    def q_own(p):
        return wq.at[pl.ds(pl.multiple_of(c * part + p * q_sub, 16), q_sub)]

    def o_own(p):
        return wo.at[pl.ds(pl.multiple_of(core * half + p * o_sub, 16), o_sub)]

    v_sub = rows // V_PARTS

    def v_out(p):
        src = video.at[pl.ds(p * v_sub, v_sub)]
        dst = vid2.at[pl.ds(pl.multiple_of(y * rows + p * v_sub, 16), v_sub)]
        return remote(src, dst, vs.at[p], vr.at[p], blk, yp)

    def v_in(p):
        r = vid2.at[pl.ds(pl.multiple_of((1 - y) * rows + p * v_sub, 16), v_sub)]
        return remote(r, r, vs.at[p], vr.at[p], blk, yp)

    onward = (uly + 2, uly - 2)
    can_go = (a < last, a > 0)

    def has(d, t):
        return (a >= t) if d == 0 else (a + t <= last)

    def came(d, t):
        return (a - t) if d == 0 else (a + t)

    def q_on(d, t, p):
        dst = q_at(came(d, t), c, p)
        k = t * Q_PARTS + p
        return remote(q_own(p) if t == 0 else dst, dst, zs.at[d, k], zr.at[d, k], blk, onward[d])

    def q_copy(d, t, p, piece, send, recv, to_blk, to_uly):
        r = q_at(came(d, t), piece, p)
        k = (t - 1) * Q_PARTS + p
        return remote(r, r, send.at[d, k], recv.at[d, k], to_blk, to_uly)

    def q_in(d, t, p):
        return q_copy(d, t, p, c, zs, zr, blk, yp)

    def q_x(d, t, p):
        return q_copy(d, t, p, c, xs, xr, xp, uly)

    def q_xin(d, t, p):
        return q_copy(d, t, p, x_c, xs, xr, xp, uly)

    def q_c(d, t, p):
        return q_copy(d, t, p, c, cs, cr, cp, uly)

    def q_cin(d, t, p):
        return q_copy(d, t, p, c + 1 - 2 * core, cs, cr, cp, uly)

    def q_d(d, t, p):
        return q_copy(d, t, p, x_c, ds, dr, cp, uly)

    def q_din(d, t, p):
        return q_copy(d, t, p, x_c + 1 - 2 * core, ds, dr, cp, uly)

    def o_copy(d, t, p, slot, side, send, recv, to_blk, to_uly, own=False):
        r = o_at(slot, side, p)
        k = t * O_PARTS + p
        return remote(o_own(p) if own else r, r, send.at[d, k], recv.at[d, k], to_blk, to_uly)

    def o_on(d, t, p):
        return o_copy(d, t, p, came(d, t) * 2 + y, core, ozs, ozr, blk, onward[d], t == 0)

    def o_in(d, t, p):
        return o_copy(d, t - 1, p, came(d, t) * 2 + y, core, ozs, ozr, blk, yp)

    def o_y(d, t, p):
        return o_copy(d, t, p, came(d, t) * 2 + y, core, oys, oyr, blk, yp, t == 0)

    def o_yin(d, t, p):
        return o_copy(d, t, p, came(d, t) * 2 + 1 - y, core, oys, oyr, blk, yp)

    def o_c(d, t, p):
        return o_copy(d, t, p, came(d, t) * 2 + y, core, ocs, ocr, cp, uly)

    def o_cin(d, t, p):
        return o_copy(d, t, p, came(d, t) * 2 + y, 1 - core, ocs, ocr, cp, uly)

    def o_d(d, t, p):
        return o_copy(d, t, p, came(d, t) * 2 + 1 - y, core, ods, odr, cp, uly)

    def o_din(d, t, p):
        return o_copy(d, t, p, came(d, t) * 2 + 1 - y, 1 - core, ods, odr, cp, uly)

    def q_arrive(d, t, p):
        q_in(d, t, p).wait_recv()
        if t < last:
            when(can_go[d], lambda: q_on(d, t, p).start())
        q_x(d, t, p).start()
        q_c(d, t, p).start()

    def q_cross(d, t, p):
        q_xin(d, t, p).wait_recv()
        q_d(d, t, p).start()

    def o_arrive(d, t, p):
        o_in(d, t, p).wait_recv()
        if t < last:
            when(can_go[d], lambda: o_on(d, t, p).start())
        o_y(d, t, p).start()
        o_c(d, t, p).start()

    def o_cross(d, t, p):
        o_yin(d, t, p).wait_recv()
        o_d(d, t, p).start()

    def each(cond, parts, fn):
        def body():
            for p in range(parts):
                fn(p)

        when(cond, body)

    for p in range(Q_PARTS):
        for d in range(2):
            when(can_go[d], lambda d=d, p=p: q_on(d, 0, p).start())
    for p in range(V_PARTS):
        v_out(p).start()
    for p in range(O_PARTS):
        o_y(0, 0, p).start()
    y_rows = pl.ds(pl.multiple_of(y * rows, 16), rows)
    mine = through_vmem(
        (wq, video, wo),
        (wq_all.at[a], vid2.at[y_rows], wo_all.at[uly]),
        (wq_v, video_v, wo_v),
        local_sem,
    )

    for t in range(1, last + 1):
        for p in range(Q_PARTS):
            for d in range(2):
                when(has(d, t), lambda d=d, p=p, t=t: q_arrive(d, t, p))
            if t > 1:
                for d in range(2):
                    when(has(d, t - 1), lambda d=d, p=p, t=t: q_cross(d, t - 1, p))
        if t == last:
            for p in range(O_PARTS):
                for d in range(2):
                    when(can_go[d], lambda d=d, p=p: o_on(d, 0, p).start())
    for p in range(O_PARTS):
        o_cross(0, 0, p)
    for d in range(2):
        each(has(d, last), Q_PARTS, lambda p, d=d: q_cross(d, last, p))
    for t in range(1, last + 1):
        for p in range(O_PARTS):
            for d in range(2):
                when(has(d, t), lambda d=d, p=p, t=t: o_arrive(d, t, p))
            if t > 1:
                for d in range(2):
                    when(has(d, t - 1), lambda d=d, p=p, t=t: o_cross(d, t - 1, p))
    for d in range(2):
        each(has(d, last), O_PARTS, lambda p, d=d: o_cross(d, last, p))

    for copy in mine:
        copy.wait()
    for p in range(V_PARTS):
        v_out(p).wait_send()
        v_in(p).wait_recv()
    for p in range(O_PARTS):
        o_y(0, 0, p).wait_send()
        o_d(0, 0, p).wait_send()
        o_din(0, 0, p).wait_recv()

    def q_end(d, t, p):
        q_x(d, t, p).wait_send()
        q_c(d, t, p).wait_send()
        q_d(d, t, p).wait_send()
        q_cin(d, t, p).wait_recv()
        q_din(d, t, p).wait_recv()

    def o_end(d, t, p):
        o_y(d, t, p).wait_send()
        o_c(d, t, p).wait_send()
        o_d(d, t, p).wait_send()
        o_cin(d, t, p).wait_recv()
        o_din(d, t, p).wait_recv()

    for d in range(2):
        for t in range(last):
            on = can_go[d] if t == 0 else jnp.logical_and(has(d, t), can_go[d])
            each(on, Q_PARTS, lambda p, d=d, t=t: q_on(d, t, p).wait_send())
            each(on, O_PARTS, lambda p, d=d, t=t: o_on(d, t, p).wait_send())
        for t in range(1, last + 1):
            each(has(d, t), Q_PARTS, lambda p, d=d, t=t: q_end(d, t, p))
            each(has(d, t), O_PARTS, lambda p, d=d, t=t: o_end(d, t, p))


def gather_weights(video, wq, wo, groups):
    rows = video.shape[0]
    q_sems = pltpu.SemaphoreType.DMA((2, groups * Q_PARTS))
    o_sems = pltpu.SemaphoreType.DMA((2, groups * O_PARTS))
    return pl.pallas_call(
        functools.partial(gather_kernel, groups),
        out_shape=(
            jax.ShapeDtypeStruct((2 * rows, video.shape[1]), video.dtype),
            jax.ShapeDtypeStruct((groups,) + wq.shape, wq.dtype),
            jax.ShapeDtypeStruct((2 * groups,) + wo.shape, wo.dtype),
        ),
        in_specs=[ANY] * 3,
        out_specs=(ANY,) * 3,
        scratch_shapes=[
            pltpu.SemaphoreType.DMA((6,)),
            pltpu.SemaphoreType.DMA((V_PARTS,)),
            pltpu.SemaphoreType.DMA((V_PARTS,)),
        ]
        + [q_sems] * 8
        + [o_sems] * 8
        + [pltpu.VMEM(block.shape, block.dtype) for block in (wq, video, wo)],
        compiler_params=pltpu.CompilerParams(
            collective_id=0, has_side_effects=True, vmem_limit_bytes=48 << 20
        ),
    )(video, wq, wo)


def exchange_kernel(groups, slabs, q, kv, q_all, kv_all, local_sem, qs, qr, ks, kr, ps, pr, ns, nr, q_v, kv_v):
    blk, uly = lax.axis_index("blk"), lax.axis_index("uly")
    a, y = uly // 2, uly % 2
    has_prev, has_next = blk > 0, blk < slabs - 1

    barrier = pltpu.get_barrier_semaphore()

    def greet(b, u):
        pl.semaphore_signal(barrier, inc=1, device_id=(b, u), device_id_type=MESH)

    for k in range(1, groups):
        greet(blk, ((a + k) % groups) * 2 + y)
    when(has_prev, lambda: greet(blk - 1, uly))
    when(has_next, lambda: greet(blk + 1, uly))
    pl.semaphore_wait(
        barrier, groups - 1 + has_prev.astype(jnp.int32) + has_next.astype(jnp.int32)
    )

    def there(k):
        return (a + k) % groups

    def source(k):
        return (a - k + groups) % groups

    def kv_out(k):
        return remote(
            kv.at[there(k)], kv_all.at[1, a], ks.at[k], kr.at[k], blk, there(k) * 2 + y
        )

    def q_out(k):
        return remote(q.at[there(k)], q_all.at[a], qs.at[k], qr.at[k], blk, there(k) * 2 + y)

    def kv_in(k):
        r = kv_all.at[1, source(k)]
        return remote(r, r, ks.at[k], kr.at[k], blk, there(k) * 2 + y)

    def q_in(k):
        r = q_all.at[source(k)]
        return remote(r, r, qs.at[k], qr.at[k], blk, there(k) * 2 + y)

    def to_prev(k):
        src = kv.at[a] if k == 0 else kv_all.at[1, source(k)]
        return remote(src, kv_all.at[2, source(k)], ps.at[k], pr.at[k], blk - 1, uly)

    def to_next(k):
        src = kv.at[a] if k == 0 else kv_all.at[1, source(k)]
        return remote(src, kv_all.at[0, source(k)], ns.at[k], nr.at[k], blk + 1, uly)

    def from_prev(k):
        r = kv_all.at[0, source(k)]
        return remote(r, r, ns.at[k], nr.at[k], blk - 1, uly)

    def from_next(k):
        r = kv_all.at[2, source(k)]
        return remote(r, r, ps.at[k], pr.at[k], blk + 1, uly)

    for k in range(1, groups):
        kv_out(k).start()
    when(has_prev, lambda: to_prev(0).start())
    when(has_next, lambda: to_next(0).start())
    for k in range(1, groups):
        q_out(k).start()
    mine = through_vmem(
        (q.at[a], kv.at[a]), (q_all.at[a], kv_all.at[1, a]), (q_v, kv_v), local_sem
    )
    for k in range(1, groups):
        kv_in(k).wait_recv()
        when(has_prev, lambda k=k: to_prev(k).start())
        when(has_next, lambda k=k: to_next(k).start())
    for copy in mine:
        copy.wait()
    for k in range(1, groups):
        kv_out(k).wait_send()
        q_out(k).wait_send()
        q_in(k).wait_recv()
    for k in range(groups):

        def prev_done(k=k):
            to_prev(k).wait_send()
            from_prev(k).wait_recv()

        def next_done(k=k):
            to_next(k).wait_send()
            from_next(k).wait_recv()

        when(has_prev, prev_done)
        when(has_next, next_done)


def exchange_heads(q, kv, groups, slabs):
    sems = pltpu.SemaphoreType.DMA((groups,))
    return pl.pallas_call(
        functools.partial(exchange_kernel, groups, slabs),
        out_shape=(
            jax.ShapeDtypeStruct(q.shape, q.dtype),
            jax.ShapeDtypeStruct((3,) + kv.shape, kv.dtype),
        ),
        in_specs=[ANY] * 2,
        out_specs=(ANY,) * 2,
        scratch_shapes=[pltpu.SemaphoreType.DMA((4,))]
        + [sems] * 8
        + [pltpu.VMEM(block.shape[1:], block.dtype) for block in (q, kv)],
        compiler_params=pltpu.CompilerParams(
            collective_id=1, has_side_effects=True, vmem_limit_bytes=48 << 20
        ),
    )(q, kv)


def attend_kernel(head_size, ids, counts, q_ref, kv_ref, out_ref, keys):
    t = pl.program_id(0)
    count = counts[t]
    chunks = (count + CHUNK - 1) // CHUNK
    slots = ids.shape[1]

    def run(n):
        width = n * CHUNK * BLOCK
        for s in range(n * CHUNK):
            tile = ids[t, s]
            keys[s * BLOCK : (s + 1) * BLOCK, :] = kv_ref[
                pl.ds(pl.multiple_of(tile * BLOCK, BLOCK), BLOCK), :
            ]
        scores = lax.dot_general(
            q_ref[...],
            keys[:width, :head_size],
            (((1,), (1,)), ((), ())),
            preferred_element_type=jnp.float32,
        )
        column = lax.broadcasted_iota(jnp.int32, scores.shape, 1)
        scores = jnp.where(column < count * BLOCK, scores, -jnp.inf)
        largest = jnp.max(scores, axis=-1, keepdims=True)
        weights = jnp.exp(scores - largest)
        total = jnp.sum(weights, axis=-1, keepdims=True)
        summed = jnp.dot(
            weights.astype(jnp.bfloat16),
            keys[:width, head_size:],
            preferred_element_type=jnp.float32,
        )
        out_ref[...] = (summed / total).astype(jnp.bfloat16)

    for n in range(1, slots // CHUNK + 1):
        when(chunks == n, lambda n=n: run(n))


def attend(q, kv, ids, counts):
    rows, head_size = q.shape
    return pl.pallas_call(
        functools.partial(attend_kernel, head_size),
        out_shape=jax.ShapeDtypeStruct(q.shape, jnp.bfloat16),
        grid_spec=pltpu.PrefetchScalarGridSpec(
            num_scalar_prefetch=2,
            grid=(rows // BLOCK,),
            in_specs=[
                pl.BlockSpec((BLOCK, head_size), lambda t, i, n: (t, 0)),
                pl.BlockSpec(kv.shape, lambda t, i, n: (0, 0)),
            ],
            out_specs=pl.BlockSpec((BLOCK, head_size), lambda t, i, n: (t, 0)),
            scratch_shapes=[pltpu.VMEM((ids.shape[1] * BLOCK, 2 * head_size), jnp.bfloat16)],
        ),
        compiler_params=pltpu.CompilerParams(vmem_limit_bytes=32 << 20),
    )(ids, counts, q, kv)


def norm_rows(values_in, gain):
    return (
        values_in
        * lax.rsqrt(jnp.mean(values_in * values_in, axis=-1, keepdims=True) + 1e-06)
        * gain
    )


def local(video, w_qkv, w_out, q_gain, k_gain, tile_blocks, tile_counts):
    head_size = w_out.shape[0]
    ranks, slabs = lax.axis_size("uly"), lax.axis_size("blk")
    groups = ranks // 2
    slab_rows = video.shape[0] * ranks
    tiles = slab_rows // BLOCK
    rows2, w_all, wo_all = gather_weights(video, w_qkv, w_out, groups)
    projected = jnp.einsum("td,adn->atn", rows2, w_all, preferred_element_type=jnp.float32)
    queries = (norm_rows(projected[..., :head_size], q_gain) * head_size ** (-0.5)).astype(
        jnp.bfloat16
    )
    keys_now = norm_rows(projected[..., head_size : 2 * head_size], k_gain).astype(jnp.bfloat16)
    values_now = projected[..., 2 * head_size :].astype(jnp.bfloat16)
    key_value = jnp.concatenate([keys_now, values_now], axis=-1)
    q_all, kv_all = exchange_heads(queries, key_value, groups, slabs)
    local_ids = tile_blocks - (lax.axis_index("blk") - 1) * tiles
    slots = -(-MAXB // CHUNK) * CHUNK
    local_ids = jnp.concatenate([local_ids] + [local_ids[:, -1:]] * (slots - MAXB), axis=1)
    attended = attend(
        q_all.reshape(slab_rows, head_size),
        kv_all.reshape(3 * slab_rows, 2 * head_size),
        local_ids,
        tile_counts,
    )
    by_token = lax.all_to_all(
        attended.reshape(ranks, video.shape[0], head_size), "uly", 0, 0, tiled=True
    )
    by_token = by_token.transpose(1, 0, 2).reshape(video.shape[0], ranks * head_size)
    mixed = jnp.dot(
        by_token,
        wo_all.reshape(ranks * head_size, w_out.shape[1]),
        preferred_element_type=jnp.float32,
    )
    return mixed.astype(jnp.bfloat16)


def solution(mesh):
    return jax.shard_map(
        local,
        mesh=mesh,
        in_specs=(
            P(("blk", "uly"), None),
            P(None, "uly"),
            P("uly", None),
            P(),
            P(),
            P("blk", None),
            P("blk"),
        ),
        out_specs=P(("blk", "uly"), None),
        check_vma=False,
    )
```

```python
import functools

import jax
import jax.numpy as jnp
from jax import lax
from jax.experimental import pallas as pl
from jax.experimental.pallas import tpu as pltpu
from jax.sharding import PartitionSpec as P

MAXB = 27
BLOCK = 64
CHUNK = 4
Q_PARTS = 4
O_PARTS = 4
V_PARTS = 2
MESH = pl.DeviceIdType.MESH
ANY = pl.BlockSpec(memory_space=pl.ANY)


def remote(src, dst, send, recv, blk, uly):
    return pltpu.make_async_remote_copy(
        src_ref=src,
        dst_ref=dst,
        send_sem=send,
        recv_sem=recv,
        device_id=(blk, uly),
        device_id_type=MESH,
    )


def through_vmem(sources, targets, rooms, sems):
    count = len(sources)
    ins = [pltpu.make_async_copy(sources[i], rooms[i], sems.at[i]) for i in range(count)]
    for copy in ins:
        copy.start()
    outs = []
    for i in range(count):
        ins[i].wait()
        outs.append(pltpu.make_async_copy(rooms[i], targets[i], sems.at[count + i]))
        outs[i].start()
    return outs


def when(cond, fn):
    pl.when(cond)(fn)


def gather_kernel(
    groups,
    video,
    wq,
    wo,
    vid2,
    wq_all,
    wo_all,
    local_sem,
    vs,
    vr,
    zs,
    zr,
    xs,
    xr,
    cs,
    cr,
    ds,
    dr,
    ozs,
    ozr,
    oys,
    oyr,
    ocs,
    ocr,
    ods,
    odr,
    wq_v,
    video_v,
    wo_v,
):
    blk, uly = lax.axis_index("blk"), lax.axis_index("uly")
    a, y = uly // 2, uly % 2
    c, core = blk % 4, blk % 2
    x_c = c + 2 - 4 * (c // 2)
    xp = blk - c + x_c
    cp = blk + 1 - 2 * core
    yp = uly + 1 - 2 * y
    last = groups - 1
    rows = video.shape[0]
    part = wq.shape[0] // 4
    half = wo.shape[0] // 2

    barrier = pltpu.get_barrier_semaphore()

    def greet(b, u):
        pl.semaphore_signal(barrier, inc=1, device_id=(b, u), device_id_type=MESH)

    greet(xp, uly)
    greet(cp, uly)
    greet(blk, yp)
    when(a > 0, lambda: greet(blk, uly - 2))
    when(a < last, lambda: greet(blk, uly + 2))
    pl.semaphore_wait(barrier, 3 + (a > 0).astype(jnp.int32) + (a < last).astype(jnp.int32))

    q_sub, o_sub = part // Q_PARTS, half // O_PARTS

    def q_at(s, piece, p):
        return wq_all.at[s, pl.ds(pl.multiple_of(piece * part + p * q_sub, 16), q_sub)]

    def o_at(s, side, p):
        return wo_all.at[s, pl.ds(pl.multiple_of(side * half + p * o_sub, 16), o_sub)]

    def q_own(p):
        return wq.at[pl.ds(pl.multiple_of(c * part + p * q_sub, 16), q_sub)]

    def o_own(p):
        return wo.at[pl.ds(pl.multiple_of(core * half + p * o_sub, 16), o_sub)]

    v_sub = rows // V_PARTS

    def v_out(p):
        src = video.at[pl.ds(p * v_sub, v_sub)]
        dst = vid2.at[pl.ds(pl.multiple_of(y * rows + p * v_sub, 16), v_sub)]
        return remote(src, dst, vs.at[p], vr.at[p], blk, yp)

    def v_in(p):
        r = vid2.at[pl.ds(pl.multiple_of((1 - y) * rows + p * v_sub, 16), v_sub)]
        return remote(r, r, vs.at[p], vr.at[p], blk, yp)

    onward = (uly + 2, uly - 2)
    can_go = (a < last, a > 0)

    def has(d, t):
        return (a >= t) if d == 0 else (a + t <= last)

    def came(d, t):
        return (a - t) if d == 0 else (a + t)

    def q_on(d, t, p):
        dst = q_at(came(d, t), c, p)
        k = t * Q_PARTS + p
        return remote(q_own(p) if t == 0 else dst, dst, zs.at[d, k], zr.at[d, k], blk, onward[d])

    def q_copy(d, t, p, piece, send, recv, to_blk, to_uly):
        r = q_at(came(d, t), piece, p)
        k = (t - 1) * Q_PARTS + p
        return remote(r, r, send.at[d, k], recv.at[d, k], to_blk, to_uly)

    def q_in(d, t, p):
        return q_copy(d, t, p, c, zs, zr, blk, yp)

    def q_x(d, t, p):
        return q_copy(d, t, p, c, xs, xr, xp, uly)

    def q_xin(d, t, p):
        return q_copy(d, t, p, x_c, xs, xr, xp, uly)

    def q_c(d, t, p):
        return q_copy(d, t, p, c, cs, cr, cp, uly)

    def q_cin(d, t, p):
        return q_copy(d, t, p, c + 1 - 2 * core, cs, cr, cp, uly)

    def q_d(d, t, p):
        return q_copy(d, t, p, x_c, ds, dr, cp, uly)

    def q_din(d, t, p):
        return q_copy(d, t, p, x_c + 1 - 2 * core, ds, dr, cp, uly)

    def o_copy(d, t, p, slot, side, send, recv, to_blk, to_uly, own=False):
        r = o_at(slot, side, p)
        k = t * O_PARTS + p
        return remote(o_own(p) if own else r, r, send.at[d, k], recv.at[d, k], to_blk, to_uly)

    def o_on(d, t, p):
        return o_copy(d, t, p, came(d, t) * 2 + y, core, ozs, ozr, blk, onward[d], t == 0)

    def o_in(d, t, p):
        return o_copy(d, t - 1, p, came(d, t) * 2 + y, core, ozs, ozr, blk, yp)

    def o_y(d, t, p):
        return o_copy(d, t, p, came(d, t) * 2 + y, core, oys, oyr, blk, yp, t == 0)

    def o_yin(d, t, p):
        return o_copy(d, t, p, came(d, t) * 2 + 1 - y, core, oys, oyr, blk, yp)

    def o_c(d, t, p):
        return o_copy(d, t, p, came(d, t) * 2 + y, core, ocs, ocr, cp, uly)

    def o_cin(d, t, p):
        return o_copy(d, t, p, came(d, t) * 2 + y, 1 - core, ocs, ocr, cp, uly)

    def o_d(d, t, p):
        return o_copy(d, t, p, came(d, t) * 2 + 1 - y, core, ods, odr, cp, uly)

    def o_din(d, t, p):
        return o_copy(d, t, p, came(d, t) * 2 + 1 - y, 1 - core, ods, odr, cp, uly)

    def q_arrive(d, t, p):
        q_in(d, t, p).wait_recv()
        if t < last:
            when(can_go[d], lambda: q_on(d, t, p).start())
        q_x(d, t, p).start()
        q_c(d, t, p).start()

    def q_cross(d, t, p):
        q_xin(d, t, p).wait_recv()
        q_d(d, t, p).start()

    def o_arrive(d, t, p):
        o_in(d, t, p).wait_recv()
        if t < last:
            when(can_go[d], lambda: o_on(d, t, p).start())
        o_y(d, t, p).start()
        o_c(d, t, p).start()

    def o_cross(d, t, p):
        o_yin(d, t, p).wait_recv()
        o_d(d, t, p).start()

    def each(cond, parts, fn):
        def body():
            for p in range(parts):
                fn(p)

        when(cond, body)

    for p in range(Q_PARTS):
        for d in range(2):
            when(can_go[d], lambda d=d, p=p: q_on(d, 0, p).start())
    for p in range(V_PARTS):
        v_out(p).start()
    for p in range(O_PARTS):
        o_y(0, 0, p).start()
    y_rows = pl.ds(pl.multiple_of(y * rows, 16), rows)
    mine = through_vmem(
        (wq, video, wo),
        (wq_all.at[a], vid2.at[y_rows], wo_all.at[uly]),
        (wq_v, video_v, wo_v),
        local_sem,
    )

    for t in range(1, last + 1):
        for p in range(Q_PARTS):
            for d in range(2):
                when(has(d, t), lambda d=d, p=p, t=t: q_arrive(d, t, p))
            if t > 1:
                for d in range(2):
                    when(has(d, t - 1), lambda d=d, p=p, t=t: q_cross(d, t - 1, p))
        if t == 1:
            for p in range(O_PARTS):
                for d in range(2):
                    when(can_go[d], lambda d=d, p=p: o_on(d, 0, p).start())
    for p in range(O_PARTS):
        o_cross(0, 0, p)
    for d in range(2):
        each(has(d, last), Q_PARTS, lambda p, d=d: q_cross(d, last, p))
    for t in range(1, last + 1):
        for p in range(O_PARTS):
            for d in range(2):
                when(has(d, t), lambda d=d, p=p, t=t: o_arrive(d, t, p))
            if t > 1:
                for d in range(2):
                    when(has(d, t - 1), lambda d=d, p=p, t=t: o_cross(d, t - 1, p))
    for d in range(2):
        each(has(d, last), O_PARTS, lambda p, d=d: o_cross(d, last, p))

    for copy in mine:
        copy.wait()
    for p in range(V_PARTS):
        v_out(p).wait_send()
        v_in(p).wait_recv()
    for p in range(O_PARTS):
        o_y(0, 0, p).wait_send()
        o_d(0, 0, p).wait_send()
        o_din(0, 0, p).wait_recv()

    def q_end(d, t, p):
        q_x(d, t, p).wait_send()
        q_c(d, t, p).wait_send()
        q_d(d, t, p).wait_send()
        q_cin(d, t, p).wait_recv()
        q_din(d, t, p).wait_recv()

    def o_end(d, t, p):
        o_y(d, t, p).wait_send()
        o_c(d, t, p).wait_send()
        o_d(d, t, p).wait_send()
        o_cin(d, t, p).wait_recv()
        o_din(d, t, p).wait_recv()

    for d in range(2):
        for t in range(last):
            on = can_go[d] if t == 0 else jnp.logical_and(has(d, t), can_go[d])
            each(on, Q_PARTS, lambda p, d=d, t=t: q_on(d, t, p).wait_send())
            each(on, O_PARTS, lambda p, d=d, t=t: o_on(d, t, p).wait_send())
        for t in range(1, last + 1):
            each(has(d, t), Q_PARTS, lambda p, d=d, t=t: q_end(d, t, p))
            each(has(d, t), O_PARTS, lambda p, d=d, t=t: o_end(d, t, p))


def gather_weights(video, wq, wo, groups):
    rows = video.shape[0]
    q_sems = pltpu.SemaphoreType.DMA((2, groups * Q_PARTS))
    o_sems = pltpu.SemaphoreType.DMA((2, groups * O_PARTS))
    return pl.pallas_call(
        functools.partial(gather_kernel, groups),
        out_shape=(
            jax.ShapeDtypeStruct((2 * rows, video.shape[1]), video.dtype),
            jax.ShapeDtypeStruct((groups,) + wq.shape, wq.dtype),
            jax.ShapeDtypeStruct((2 * groups,) + wo.shape, wo.dtype),
        ),
        in_specs=[ANY] * 3,
        out_specs=(ANY,) * 3,
        scratch_shapes=[
            pltpu.SemaphoreType.DMA((6,)),
            pltpu.SemaphoreType.DMA((V_PARTS,)),
            pltpu.SemaphoreType.DMA((V_PARTS,)),
        ]
        + [q_sems] * 8
        + [o_sems] * 8
        + [pltpu.VMEM(block.shape, block.dtype) for block in (wq, video, wo)],
        compiler_params=pltpu.CompilerParams(
            collective_id=0, has_side_effects=True, vmem_limit_bytes=48 << 20
        ),
    )(video, wq, wo)


def exchange_kernel(groups, slabs, q, kv, q_all, kv_all, local_sem, qs, qr, ks, kr, ps, pr, ns, nr, q_v, kv_v):
    blk, uly = lax.axis_index("blk"), lax.axis_index("uly")
    a, y = uly // 2, uly % 2
    has_prev, has_next = blk > 0, blk < slabs - 1

    barrier = pltpu.get_barrier_semaphore()

    def greet(b, u):
        pl.semaphore_signal(barrier, inc=1, device_id=(b, u), device_id_type=MESH)

    for k in range(1, groups):
        greet(blk, ((a + k) % groups) * 2 + y)
    when(has_prev, lambda: greet(blk - 1, uly))
    when(has_next, lambda: greet(blk + 1, uly))
    pl.semaphore_wait(
        barrier, groups - 1 + has_prev.astype(jnp.int32) + has_next.astype(jnp.int32)
    )

    def there(k):
        return (a + k) % groups

    def source(k):
        return (a - k + groups) % groups

    def kv_out(k):
        return remote(
            kv.at[there(k)], kv_all.at[1, a], ks.at[k], kr.at[k], blk, there(k) * 2 + y
        )

    def q_out(k):
        return remote(q.at[there(k)], q_all.at[a], qs.at[k], qr.at[k], blk, there(k) * 2 + y)

    def kv_in(k):
        r = kv_all.at[1, source(k)]
        return remote(r, r, ks.at[k], kr.at[k], blk, there(k) * 2 + y)

    def q_in(k):
        r = q_all.at[source(k)]
        return remote(r, r, qs.at[k], qr.at[k], blk, there(k) * 2 + y)

    def to_prev(k):
        src = kv.at[a] if k == 0 else kv_all.at[1, source(k)]
        return remote(src, kv_all.at[2, source(k)], ps.at[k], pr.at[k], blk - 1, uly)

    def to_next(k):
        src = kv.at[a] if k == 0 else kv_all.at[1, source(k)]
        return remote(src, kv_all.at[0, source(k)], ns.at[k], nr.at[k], blk + 1, uly)

    def from_prev(k):
        r = kv_all.at[0, source(k)]
        return remote(r, r, ns.at[k], nr.at[k], blk - 1, uly)

    def from_next(k):
        r = kv_all.at[2, source(k)]
        return remote(r, r, ps.at[k], pr.at[k], blk + 1, uly)

    for k in range(1, groups):
        kv_out(k).start()
    when(has_prev, lambda: to_prev(0).start())
    when(has_next, lambda: to_next(0).start())
    for k in range(1, groups):
        q_out(k).start()
    mine = through_vmem(
        (q.at[a], kv.at[a]), (q_all.at[a], kv_all.at[1, a]), (q_v, kv_v), local_sem
    )
    for k in range(1, groups):
        kv_in(k).wait_recv()
        when(has_prev, lambda k=k: to_prev(k).start())
        when(has_next, lambda k=k: to_next(k).start())
    for copy in mine:
        copy.wait()
    for k in range(1, groups):
        kv_out(k).wait_send()
        q_out(k).wait_send()
        q_in(k).wait_recv()
    for k in range(groups):

        def prev_done(k=k):
            to_prev(k).wait_send()
            from_prev(k).wait_recv()

        def next_done(k=k):
            to_next(k).wait_send()
            from_next(k).wait_recv()

        when(has_prev, prev_done)
        when(has_next, next_done)


def exchange_heads(q, kv, groups, slabs):
    sems = pltpu.SemaphoreType.DMA((groups,))
    return pl.pallas_call(
        functools.partial(exchange_kernel, groups, slabs),
        out_shape=(
            jax.ShapeDtypeStruct(q.shape, q.dtype),
            jax.ShapeDtypeStruct((3,) + kv.shape, kv.dtype),
        ),
        in_specs=[ANY] * 2,
        out_specs=(ANY,) * 2,
        scratch_shapes=[pltpu.SemaphoreType.DMA((4,))]
        + [sems] * 8
        + [pltpu.VMEM(block.shape[1:], block.dtype) for block in (q, kv)],
        compiler_params=pltpu.CompilerParams(
            collective_id=1, has_side_effects=True, vmem_limit_bytes=48 << 20
        ),
    )(q, kv)


def attend_kernel(head_size, ids, counts, q_ref, kv_ref, out_ref, keys):
    t = pl.program_id(0)
    count = counts[t]
    chunks = (count + CHUNK - 1) // CHUNK
    slots = ids.shape[1]

    def run(n):
        width = n * CHUNK * BLOCK
        for s in range(n * CHUNK):
            tile = ids[t, s]
            keys[s * BLOCK : (s + 1) * BLOCK, :] = kv_ref[
                pl.ds(pl.multiple_of(tile * BLOCK, BLOCK), BLOCK), :
            ]
        scores = lax.dot_general(
            q_ref[...],
            keys[:width, :head_size],
            (((1,), (1,)), ((), ())),
            preferred_element_type=jnp.float32,
        )
        column = lax.broadcasted_iota(jnp.int32, scores.shape, 1)
        scores = jnp.where(column < count * BLOCK, scores, -jnp.inf)
        largest = jnp.max(scores, axis=-1, keepdims=True)
        weights = jnp.exp(scores - largest)
        total = jnp.sum(weights, axis=-1, keepdims=True)
        summed = jnp.dot(
            weights.astype(jnp.bfloat16),
            keys[:width, head_size:],
            preferred_element_type=jnp.float32,
        )
        out_ref[...] = (summed / total).astype(jnp.bfloat16)

    for n in range(1, slots // CHUNK + 1):
        when(chunks == n, lambda n=n: run(n))


def attend(q, kv, ids, counts):
    rows, head_size = q.shape
    return pl.pallas_call(
        functools.partial(attend_kernel, head_size),
        out_shape=jax.ShapeDtypeStruct(q.shape, jnp.bfloat16),
        grid_spec=pltpu.PrefetchScalarGridSpec(
            num_scalar_prefetch=2,
            grid=(rows // BLOCK,),
            in_specs=[
                pl.BlockSpec((BLOCK, head_size), lambda t, i, n: (t, 0)),
                pl.BlockSpec(kv.shape, lambda t, i, n: (0, 0)),
            ],
            out_specs=pl.BlockSpec((BLOCK, head_size), lambda t, i, n: (t, 0)),
            scratch_shapes=[pltpu.VMEM((ids.shape[1] * BLOCK, 2 * head_size), jnp.bfloat16)],
        ),
        compiler_params=pltpu.CompilerParams(vmem_limit_bytes=32 << 20),
    )(ids, counts, q, kv)


def norm_rows(values_in, gain):
    return (
        values_in
        * lax.rsqrt(jnp.mean(values_in * values_in, axis=-1, keepdims=True) + 1e-06)
        * gain
    )


def local(video, w_qkv, w_out, q_gain, k_gain, tile_blocks, tile_counts):
    head_size = w_out.shape[0]
    ranks, slabs = lax.axis_size("uly"), lax.axis_size("blk")
    groups = ranks // 2
    slab_rows = video.shape[0] * ranks
    tiles = slab_rows // BLOCK
    rows2, w_all, wo_all = gather_weights(video, w_qkv, w_out, groups)
    projected = jnp.einsum("td,adn->atn", rows2, w_all, preferred_element_type=jnp.float32)
    queries = (norm_rows(projected[..., :head_size], q_gain) * head_size ** (-0.5)).astype(
        jnp.bfloat16
    )
    keys_now = norm_rows(projected[..., head_size : 2 * head_size], k_gain).astype(jnp.bfloat16)
    values_now = projected[..., 2 * head_size :].astype(jnp.bfloat16)
    key_value = jnp.concatenate([keys_now, values_now], axis=-1)
    q_all, kv_all = exchange_heads(queries, key_value, groups, slabs)
    local_ids = tile_blocks - (lax.axis_index("blk") - 1) * tiles
    slots = -(-MAXB // CHUNK) * CHUNK
    local_ids = jnp.concatenate([local_ids] + [local_ids[:, -1:]] * (slots - MAXB), axis=1)
    attended = attend(
        q_all.reshape(slab_rows, head_size),
        kv_all.reshape(3 * slab_rows, 2 * head_size),
        local_ids,
        tile_counts,
    )
    by_token = lax.all_to_all(
        attended.reshape(ranks, video.shape[0], head_size), "uly", 0, 0, tiled=True
    )
    by_token = by_token.transpose(1, 0, 2).reshape(video.shape[0], ranks * head_size)
    mixed = jnp.dot(
        by_token,
        wo_all.reshape(ranks * head_size, w_out.shape[1]),
        preferred_element_type=jnp.float32,
    )
    return mixed.astype(jnp.bfloat16)


def solution(mesh):
    return jax.shard_map(
        local,
        mesh=mesh,
        in_specs=(
            P(("blk", "uly"), None),
            P(None, "uly"),
            P("uly", None),
            P(),
            P(),
            P("blk", None),
            P("blk"),
        ),
        out_specs=P(("blk", "uly"), None),
        check_vma=False,
    )
```
